256 devices in a mesh: cuts: 2 (over z_lo), dev: 128 (over y, z_hi, x, core).
Axes of the slice: x: 4, y: 4, z: 8 (z_hi: 4, z_lo: 2; z = z_hi * 2 + z_lo), core: 2. Of those that a mesh axis runs over, the one named last changes fastest.
Arguments:
- resp_q: bfloat16 [131072, 2048], P(('cuts', 'dev')), may hold values from -64 to 64, as said below
- resp_kv: bfloat16 [131072, 1024], P(('cuts', 'dev')), may hold values from -6 to 6
- resp_out_grad: bfloat16 [131072, 2048], P(('cuts', 'dev')), may hold values from -6 to 6
- resp_x: bfloat16 [131072, 4096], P(('cuts', 'dev')), may hold values from -24 to 24
- prompt_kv: bfloat16 [32768, 1024], P(('cuts', 'dev')), may hold values from -6 to 6
- stretch_offset: int32 [2048], P(('cuts', 'dev')), may hold values from -2 to 2
Outputs:
- prompt_kv_grad: float32 [32768, 1024], P(('cuts', 'dev'))
- kv_weight_grad: float32 [4096, 1024], P('dev')
The draws below stay inside these ranges and needn't reach their ends.
Inputs may be any that keep to these rules, and one draw needn't show every extreme that they name: `stretch_offset`: each entry lies between -2 and 2; counts per prompt are uneven. `resp_q`: queries are real-valued; a few rows are much larger than the rest.
All inputs are finite; a program needn't handle non-finite values.
Results may differ from the reference program's by a relative error of at most 0.012.
Values may be sent and summed in bfloat16 or wider, within the bound.
A program may use at most 128 MiB of HBM per device.

```python
import jax
import jax.numpy as jnp
from jax import lax

D = 4096
QH = 16
KVH = 4
HD = 128
PLEN = 128
STRETCH = 64
CH_DEV = 8
REACH = 2
TOK_DEV = 512
KVW = 1024
PROMPTS = 256
TOKENS = 131072
N_CUTS = 2
N_DEV = 128


def draw_resp_q(key, part):
    key = jax.random.fold_in(key, 11)
    values = jnp.clip(jax.random.normal(key, (TOKENS, QH * HD), jnp.float32), -6.0, 6.0)
    rows = jnp.arange(TOKENS)
    boost = jnp.where(rows % 61 == 0, 12.0, 1.0)
    values = jnp.clip(values * boost[:, None], -64.0, 64.0)
    return values.astype(jnp.bfloat16)


def touch_ends(result, own_key, least, largest):
    longest = result.shape.index(max(result.shape))
    spots = []
    for shift in (0, 1):
        where = [jax.random.randint(jax.random.fold_in(own_key, axis), (), 0, length) for axis, length in enumerate(result.shape)]
        where[longest] = (where[longest] + shift) % result.shape[longest]
        spots.append(tuple(where))
    return result.at[spots[0]].set(least).at[spots[1]].set(largest)


def spiked(array, key, source, target, blocks, factor):
    owner, partner = [(jnp.arange(array.shape[position]) // (array.shape[position] // blocks)).reshape([-1 if axis == position else 1 for axis in range(array.ndim)]) for position in (source, target)]
    chosen = jax.random.permutation(key, blocks)[partner]
    strong = (owner == chosen) | (owner == (partner + blocks // 2) % blocks)
    return jnp.where(strong, factor * array, array)


def level_of(own_key, shape, shards, least, top_value):
    def one(axis_at, shards_of):
        draws = jax.random.uniform(jax.random.fold_in(jax.random.fold_in(own_key, 6), axis_at), (shards_of,), jnp.float32, least / len(shards), top_value / len(shards))
        return jnp.repeat(jnp.exp(draws), shape[axis_at] // shards_of).reshape((-1,) + (1,) * (len(shape) - axis_at - 1))

    gain = one(*shards[0])
    for cut in shards[1:]:
        gain = gain * one(*cut)
    return gain


def normal_values(key, shape, spread, bound, split=(), held_as=jnp.bfloat16):
    array = jax.random.normal(key, shape, jnp.float32) * spread
    if len(split) > 0:
        array = level_of(key, shape, split, -0.22, 0.18) * array
    return jnp.clip(array, min=-bound, max=bound).astype(held_as)


def noise_with(stream_key, shape, scale, most, pieces, heavy, held_as=jnp.bfloat16):
    drawn = scale * jax.random.normal(stream_key, shape, jnp.float32)
    if pieces:
        drawn = drawn * level_of(stream_key, shape, pieces, -0.22, 0.18)
    return jnp.clip(spiked(drawn, jax.random.fold_in(stream_key, 3), *heavy), -most, most).astype(held_as)


def setup_inputs(seed: int = 0) -> dict:
    key_of = jax.random.split(jax.random.key(seed), 7)
    resp_q = draw_resp_q(jax.random.fold_in(key_of[6], 71), 0)
    resp_kv = normal_values(key_of[1], (TOKENS, KVW), 1.0, 6.0, ((0, 256),))
    resp_out_grad = normal_values(key_of[2], (TOKENS, QH * HD), 1.0, 6.0, ((0, 256),))
    resp_x = noise_with(key_of[3], (TOKENS, D), 1.0, 24.0, ((0, 256),), (0, 1, 256, 6.0))
    prompt_kv = normal_values(key_of[4], (PROMPTS * PLEN, KVW), 1.0, 6.0, ((0, 256),))
    stretch_offset = touch_ends(jax.random.randint(key_of[5], (PROMPTS * CH_DEV,), 0 - REACH, REACH + 1), jax.random.fold_in(key_of[5], 1), 0 - REACH, REACH).astype(jnp.int32)
    return dict(resp_q=resp_q, resp_kv=resp_kv, resp_out_grad=resp_out_grad, resp_x=resp_x, prompt_kv=prompt_kv, stretch_offset=stretch_offset)


def block_terms(queries, own_kv, out_grad, chosen):
    count = queries.shape[0]
    group = QH // KVH
    half = KVH * HD
    span = PLEN + STRETCH
    keys = jnp.concatenate([chosen[:, :, :half], own_kv[:, :, :half]], axis=1).reshape(count, span, KVH, HD).astype(jnp.float32)
    values = jnp.concatenate([chosen[:, :, half:], own_kv[:, :, half:]], axis=1).reshape(count, span, KVH, HD).astype(jnp.float32)
    qq = queries.reshape(count, STRETCH, KVH, group, HD).astype(jnp.float32)
    dout = out_grad.reshape(count, STRETCH, KVH, group, HD).astype(jnp.float32)
    scale = HD ** -0.5
    scores = jnp.einsum('cikgd,cjkd->ckgij', qq, keys) * scale
    keypos = jnp.arange(span)
    qpos = jnp.arange(STRETCH)
    visible = (keypos[None, :] < PLEN) | (keypos[None, :] - PLEN <= qpos[:, None])
    scores = jnp.where(visible, scores, -1e30)
    top = jnp.max(scores, axis=-1, keepdims=True)
    expo = jnp.exp(scores - top)
    probs = expo / jnp.sum(expo, axis=-1, keepdims=True)
    probs_b = probs.astype(jnp.bfloat16).astype(jnp.float32)
    out = jnp.einsum('ckgij,cjkd->cikgd', probs_b, values)
    rowdot = jnp.sum(dout * out, axis=-1)
    dprobs = jnp.einsum('cikgd,cjkd->ckgij', dout, values)
    dscores = probs * (dprobs - jnp.transpose(rowdot, (0, 2, 3, 1))[..., None])
    dscores_b = dscores.astype(jnp.bfloat16).astype(jnp.float32)
    kgrad = jnp.einsum('ckgij,cikgd->cjkd', dscores_b, qq) * scale
    vgrad = jnp.einsum('ckgij,cikgd->cjkd', probs_b, dout)
    return jnp.concatenate([kgrad.reshape(count, span, half), vgrad.reshape(count, span, half)], axis=-1)


def reference(resp_q, resp_kv, resp_out_grad, resp_x, prompt_kv, stretch_offset):
    devices = N_CUTS * N_DEV
    prompt_blocks = prompt_kv.reshape(devices, PLEN, KVW)
    inputs = (resp_q.reshape(devices, CH_DEV, STRETCH, QH * HD),
              resp_kv.reshape(devices, CH_DEV, STRETCH, KVW),
              resp_out_grad.reshape(devices, CH_DEV, STRETCH, QH * HD),
              resp_x.reshape(devices, TOK_DEV, D),
              stretch_offset.reshape(devices, CH_DEV),
              jnp.arange(devices, dtype=jnp.int32))

    def step(carry, item):
        prompt_acc, weight_acc = carry
        queries, own_kv, out_grad, rows_x, offsets, device = item
        cut = device // N_DEV
        local = device % N_DEV
        owners = (cut * N_DEV + jnp.mod(local - offsets, N_DEV)).astype(jnp.int32)
        chosen = prompt_blocks[owners]
        terms = block_terms(queries, own_kv, out_grad, chosen)
        prompt_acc = prompt_acc.at[owners].add(terms[:, :PLEN])
        resp_grad_b = terms[:, PLEN:].reshape(TOK_DEV, KVW).astype(jnp.bfloat16)
        weight_acc = weight_acc + jnp.dot(rows_x.T, resp_grad_b, preferred_element_type=jnp.float32)
        return (prompt_acc, weight_acc), None

    start = (jnp.zeros((devices, PLEN, KVW), jnp.float32), jnp.zeros((D, KVW), jnp.float32))
    (prompt_acc, weight_acc), _ = lax.scan(step, start, inputs)
    prompt_kv_grad = prompt_acc.reshape(devices * PLEN, KVW)
    return prompt_kv_grad, weight_acc
```

```python
import math

import jax
import jax.numpy as jnp
from jax import lax
from jax.experimental import pallas as pl
from jax.experimental.pallas import tpu as pltpu
from jax.sharding import PartitionSpec as P

QH = 16
KVH = 4
GROUP = QH // KVH
HD = 128
PLEN = 128
STRETCH = 64
REACH = 2
KVW = 1024
HALF = KVH * HD
BLOCKS = 8
TOK = BLOCKS * STRETCH
RING = 4
TILES = 16
PAIR = 2 * HD
Z_Y = (0, 1, 2)
Z_X = (3,)
ROWS_Y = len(Z_Y) * 128
ROWS_X = len(Z_X) * 128
SHIFT = (0, 1, 2, -1, -2)
SCALE = HD ** -0.5
LOG2E = 1.4426950408889634

BF = jnp.bfloat16
F32 = jnp.float32


def remote(src, dst, send, recv, device):
    return pltpu.make_async_remote_copy(
        src_ref=src,
        dst_ref=dst,
        send_sem=send,
        recv_sem=recv,
        device_id=device,
        device_id_type=pl.DeviceIdType.MESH,
    )


def nt(a, b):
    return lax.dot_general(a, b, (((1,), (1,)), ((), ())), preferred_element_type=F32)


def nn(a, b):
    return lax.dot_general(a, b, (((1,), (0,)), ((), ())), preferred_element_type=F32)


def place_of(x, core):
    same = (x // 2 + core + 1) % 2
    to_x = same * x + (1 - same) * (3 - x)
    to_core = same * (1 - core) + (1 - same) * core
    return to_x, to_core


def source_of(x, core):
    same = (x // 2 + core + 1) % 2
    from_x = (1 - same) * x + same * (3 - x)
    from_core = (1 - same) * (1 - core) + same * core
    return from_x, from_core


def part_of(x, core):
    to_x, to_core = place_of(x, core)
    return (to_x % 2) * 2 + to_core


class Ring:
    def __init__(self, buf, near, full, far_sems, send, mine, right, left, far, to_right, to_left):
        self.buf, self.near, self.full = buf, near, full
        self.recv, self.send = far_sems, send
        self.mine, self.right, self.left, self.far = mine, right, left, far
        self.to_right, self.to_left = to_right, to_left
        self.rows = buf.shape[1]
        self.half = self.rows // 2

    def copy(self, which):
        low, high = pl.ds(0, self.half), pl.ds(self.half, self.half)
        source = (
            self.buf.at[self.far, low],
            self.buf.at[self.far, high],
            self.buf.at[self.right],
            self.buf.at[self.left],
        )[which]
        target = (self.near if which < 2 else self.full).at[which % 2]
        device = (self.to_right, self.to_left)[which % 2]
        return remote(source, target, self.send, self.recv.at[which], device)

    def first(self):
        self.copy(0).start()
        self.copy(1).start()

    def second(self):
        half = self.half
        self.copy(0).wait_recv()
        self.buf[self.right, 0:half] = (
            self.buf[self.right, 0:half].astype(F32) + self.near[0].astype(F32)
        ).astype(BF)
        self.copy(2).start()
        self.copy(1).wait_recv()
        self.buf[self.left, half:] = (
            self.buf[self.left, half:].astype(F32) + self.near[1].astype(F32)
        ).astype(BF)
        self.copy(3).start()

    def arrive(self):
        self.copy(2).wait_recv()
        self.copy(3).wait_recv()

    def total(self, rows):
        return (
            self.buf[self.mine, rows].astype(F32)
            + self.full[0, rows].astype(F32)
            + self.full[1, rows].astype(F32)
        )

    def sent(self):
        whole = self.buf.at[pl.ds(0, 3)]
        remote(whole, whole, self.send, self.recv.at[0], self.to_right).wait_send()


def kernel(
    off_ref, q_hbm, kv_hbm, do_hbm, x_hbm, p_hbm, outp_ref, outw_ref,
    q_v, do_v, kv_v, xo_v, xp_v, xt_v, pk0, pk1, pk2, pk3, tb, po, g_v, sb, rb,
    wy, wy_near, wy_full, wx, wx_near, wx_full,
    vy, vy_near, vy_full, vx, vx_near, vx_full, zs, zr,
    load_sem, psend, precv, xsend, xrecv, gsend, grecv, tsend, trecv, zsend, zrecv,
    rsend, rrecv,
):
    cut = lax.axis_index("cuts")
    dev = lax.axis_index("dev")
    count = lax.axis_size("dev")
    core = dev % 2
    x = (dev // 2) % RING
    zh = (dev // 8) % RING
    y = dev // 32
    pk = (pk0, pk1, pk2, pk3)

    def at(y_, zh_, x_, core_):
        return ((y_ * RING + zh_) * RING + x_) * 2 + core_

    partner = (cut, at(y, zh, x, 1 - core))
    x_right, x_left = (cut, at(y, zh, (x + 1) % RING, core)), (cut, at(y, zh, (x + 3) % RING, core))
    y_right, y_left = (cut, at((y + 1) % RING, zh, x, core)), (cut, at((y + 3) % RING, zh, x, core))
    to_x, to_core = place_of(x, core)
    from_x, from_core = source_of(x, core)

    def own_loads(h):
        cols = pl.ds(h * GROUP * HD, GROUP * HD)
        return (
            pltpu.make_async_copy(q_hbm.at[:, cols], q_v.at[h], load_sem.at[0, h]),
            pltpu.make_async_copy(do_hbm.at[:, cols], do_v.at[h], load_sem.at[1, h]),
        )

    def prompt_loads(h):
        return (
            pltpu.make_async_copy(
                p_hbm.at[:, pl.ds(h * HD, HD)], pk[h].at[0, 0], load_sem.at[2, h]
            ),
            pltpu.make_async_copy(
                p_hbm.at[:, pl.ds(HALF + h * HD, HD)], pk[h].at[0, 1], load_sem.at[3, h]
            ),
        )

    kv_load = pltpu.make_async_copy(kv_hbm, kv_v, load_sem.at[4, 0])

    @pl.loop(0, TILES)
    def _(t):
        cols = pl.ds(pl.multiple_of((t * 2 + core) * HD, HD), HD)
        pltpu.make_async_copy(x_hbm.at[:, cols], xo_v.at[t], load_sem.at[4, 1]).start()

    for h in range(KVH):
        for copy in prompt_loads(h) + own_loads(h):
            copy.start()
        if h == 0:
            kv_load.start()

    barrier = pltpu.get_barrier_semaphore()

    def greet(device):
        pl.semaphore_signal(
            barrier, inc=1, device_id=device, device_id_type=pl.DeviceIdType.MESH
        )

    for shift in SHIFT[1:]:
        greet((cut, (dev + shift + count) % count))
    for device in (partner, x_right, x_left, y_right, y_left):
        greet(device)
    for zl_ in range(2):
        for zh_ in range(RING):
            greet((zl_, at(y, zh_, from_x, from_core)))

    pltpu.make_async_copy(xo_v, xo_v, load_sem.at[4, 1]).wait()
    pl.semaphore_wait(barrier, 4 + 5 + 8)

    def prompt_sends(h, slot):
        device = (cut, (dev + SHIFT[slot] + count) % count)
        return (
            remote(
                p_hbm.at[:, pl.ds(h * HD, HD)], pk[h].at[slot, 0], psend.at[h], precv.at[h], device
            ),
            remote(
                p_hbm.at[:, pl.ds(HALF + h * HD, HD)], pk[h].at[slot, 1], psend.at[h], precv.at[h], device
            ),
        )

    for h in range(KVH):
        for slot in range(1, 5):
            for copy in prompt_sends(h, slot):
                copy.start()

    @pl.loop(0, TILES)
    def _(t):
        cols = pl.ds(pl.multiple_of((t * 2 + 1 - core) * HD, HD), HD)
        remote(x_hbm.at[:, cols], xp_v.at[t], xsend.at[0], xrecv.at[0], partner).start()

    @pl.loop(0, TILES)
    def _(t):
        xt_v[t, :, 0:TOK] = xo_v[t].T

    key_at = lax.broadcasted_iota(jnp.int32, (STRETCH, GROUP * STRETCH), 0)
    query_at = lax.broadcasted_iota(jnp.int32, (STRETCH, GROUP * STRETCH), 1) % STRETCH
    seen = key_at <= query_at

    def slot_of(c):
        off = off_ref[c]
        return jnp.where(off >= 0, off, REACH - off)

    def block(h, c):
        slot = slot_of(c)
        rows = pl.ds(pl.multiple_of(c * STRETCH, STRETCH), STRETCH)
        queries = jnp.concatenate(
            [q_v[h, rows, g * HD:(g + 1) * HD] for g in range(GROUP)], axis=0
        )
        dout = jnp.concatenate(
            [do_v[h, rows, g * HD:(g + 1) * HD] for g in range(GROUP)], axis=0
        )
        keys = jnp.concatenate([pk[h][slot, 0], kv_v[rows, h * HD:(h + 1) * HD]], axis=0)
        values = jnp.concatenate(
            [pk[h][slot, 1], kv_v[rows, HALF + h * HD:HALF + (h + 1) * HD]], axis=0
        )
        scores = nt(keys, queries)
        dprobs = nt(values, dout)
        scores = jnp.concatenate(
            [scores[:PLEN], jnp.where(seen, scores[PLEN:], -1e30)], axis=0
        )
        top = jnp.max(scores, axis=0, keepdims=True)
        expo = jnp.exp2((scores - top) * (SCALE * LOG2E))
        probs = expo * (1.0 / jnp.sum(expo, axis=0, keepdims=True))
        probs_b = probs.astype(BF)
        rowdot = jnp.sum(probs_b.astype(F32) * dprobs, axis=0, keepdims=True)
        dscores_b = (probs * (dprobs - rowdot)).astype(BF)
        kgrad = nn(dscores_b, queries) * SCALE
        vgrad = nn(probs_b, dout)
        g_v[h, rows, 0:HD] = kgrad[PLEN:].astype(BF)
        g_v[h, rows, HD:] = vgrad[PLEN:].astype(BF)
        tb[c, :, 0:HD] = kgrad[:PLEN]
        tb[c, :, HD:] = vgrad[:PLEN]

    def g_copy(h):
        return remote(
            g_v.at[h, pl.ds(0, TOK)], g_v.at[h, pl.ds(TOK, TOK)], gsend.at[h], grecv.at[h], partner
        )

    def term_copy(h, slot):
        device = (cut, (dev - SHIFT[slot] + count) % count)
        return remote(sb.at[h, slot - 1], rb.at[h, slot - 1], tsend.at[h], trecv.at[h], device)

    def attend(h):
        for copy in prompt_loads(h) + own_loads(h):
            copy.wait()
        if h == 0:
            kv_load.wait()
        arrived = pk[h].at[pl.ds(1, 4)]
        remote(arrived, arrived, psend.at[h], precv.at[h], partner).wait_recv()

        @pl.loop(0, BLOCKS // 2)
        def _(i):
            block(h, i * 2)
            block(h, i * 2 + 1)

        g_copy(h).start()

        slots = [slot_of(c) for c in range(BLOCKS)]

        @pl.loop(0, PLEN // 16)
        def _(i):
            rows = pl.ds(pl.multiple_of(i * 16, 16), 16)
            sums = [jnp.zeros((16, PAIR), F32) for _ in SHIFT]
            for c in range(BLOCKS):
                term = tb[c, rows]
                for n in range(len(SHIFT)):
                    sums[n] = sums[n] + jnp.where(slots[c] == n, term, 0.0)
            po[h, rows] = sums[0]
            for n in range(1, len(SHIFT)):
                sb[h, n - 1, rows] = sums[n].astype(BF)

        for slot in range(1, 5):
            term_copy(h, slot).start()

    def ring_y(h):
        return Ring(
            wy.at[h], wy_near.at[h], wy_full.at[h], rrecv.at[h, 0], rsend.at[h, 0],
            y, (y + 1) % RING, (y + 3) % RING, (y + 2) % RING, y_right, y_left,
        )

    def ring_x(h):
        return Ring(
            wx.at[h], wx_near.at[h], wx_full.at[h], rrecv.at[h, 1], rsend.at[h, 1],
            part_of(x, core), part_of((x + 1) % RING, core), part_of((x + 3) % RING, core),
            part_of((x + 2) % RING, core), x_right, x_left,
        )

    def ring_y2(h):
        return Ring(
            vx.at[h], vx_near.at[h], vx_full.at[h], rrecv.at[h, 2], rsend.at[h, 2],
            y, (y + 1) % RING, (y + 3) % RING, (y + 2) % RING, y_right, y_left,
        )

    def ring_x2(h):
        return Ring(
            vy.at[h], vy_near.at[h], vy_full.at[h], rrecv.at[h, 3], rsend.at[h, 3],
            part_of(x, core), part_of((x + 1) % RING, core), part_of((x + 3) % RING, core),
            part_of((x + 2) % RING, core), x_right, x_left,
        )

    def product(h):
        g_copy(h).wait_recv()

        def chunk(step):
            to = (y + 2 + step) % RING
            left = xt_v[pl.ds(to * RING, RING)].reshape(RING * 128, 2 * TOK)
            out = nn(left, g_v[h]).astype(BF)
            for place, z in enumerate(Z_Y):
                wy[h, to, place * 128:(place + 1) * 128] = out[z * 128:(z + 1) * 128]
            for place, z in enumerate(Z_X):
                for k in range(RING):
                    row = pl.multiple_of(to * (ROWS_X // RING) + place * 32, 32)
                    wx[h, k, pl.ds(row, 32)] = out[z * 128 + k * 32:z * 128 + (k + 1) * 32]

        chunk(0)
        ring_y(h).first()

        @pl.loop(1, RING)
        def _(step):
            chunk(step)

        ring_x(h).first()

    def second(h):
        ring_y(h).second()
        ring_x(h).second()

    def third(h):
        ring = ring_y(h)
        ring.arrive()
        for place in range(len(Z_Y)):
            for k in range(RING):
                row = place * 128 + k * 32
                vy[h, k, place * 32:(place + 1) * 32] = ring.total(pl.ds(row, 32)).astype(BF)
        ring_x2(h).first()
        ring = ring_x(h)
        ring.arrive()
        for k in range(RING):
            vx[h, k] = ring.total(pl.ds(k * (ROWS_X // RING), ROWS_X // RING)).astype(BF)
        ring_y2(h).first()

    def fourth(h):
        ring_x2(h).second()
        ring_y2(h).second()

    def z_copy(h, zl_, zh_):
        return remote(
            zs.at[h, zh_], zr.at[h, zh * 2 + cut], zsend.at[h], zrecv.at[h],
            (zl_, at(y, zh_, to_x, to_core)),
        )

    def fifth(h):
        ring = ring_x2(h)
        ring.arrive()
        for place, z in enumerate(Z_Y):
            zs[h, z] = ring.total(pl.ds(place * 32, 32)).astype(BF)
        ring = ring_y2(h)
        ring.arrive()
        for place, z in enumerate(Z_X):
            zs[h, z] = ring.total(pl.ds(place * 32, 32)).astype(BF)
        for zh_ in range(RING):
            for zl_ in range(2):
                z_copy(h, zl_, zh_).start()

    def last(h):
        remote(zr.at[h], zr.at[h], zsend.at[h], zrecv.at[h], partner).wait_recv()
        done = zr[h, 0].astype(F32)
        for source in range(1, 8):
            done = done + zr[h, source].astype(F32)
        outw_ref[:, h * HD:(h + 1) * HD] = done[:, :HD]
        outw_ref[:, HALF + h * HD:HALF + (h + 1) * HD] = done[:, HD:]

    def prompt_last(h):
        remote(rb.at[h], rb.at[h], tsend.at[h], trecv.at[h], partner).wait_recv()

        @pl.loop(0, PLEN // 32)
        def _(i):
            rows = pl.ds(pl.multiple_of(i * 32, 32), 32)
            done = po[h, rows]
            for n in range(4):
                done = done + rb[h, n, rows].astype(F32)
            outp_ref[rows, h * HD:(h + 1) * HD] = done[:, :HD]
            outp_ref[rows, HALF + h * HD:HALF + (h + 1) * HD] = done[:, HD:]

    attend(0)
    remote(xp_v, xp_v, xsend.at[0], xrecv.at[0], partner).wait_recv()

    @pl.loop(0, TILES)
    def _(t):
        xt_v[t, :, TOK:] = xp_v[t].T

    product(0)
    attend(1)
    second(0)
    product(1)
    attend(2)
    third(0)
    second(1)
    product(2)
    attend(3)
    fourth(0)
    third(1)
    second(2)
    product(3)
    fifth(0)
    fourth(1)
    third(2)
    prompt_last(0)
    second(3)
    fifth(1)
    fourth(2)
    prompt_last(1)
    third(3)
    fifth(2)
    prompt_last(2)
    last(0)
    fourth(3)
    last(1)
    prompt_last(3)
    fifth(3)
    last(2)
    last(3)

    for h in range(KVH):
        arrived = pk[h].at[pl.ds(1, 4)]
        remote(arrived, arrived, psend.at[h], precv.at[h], partner).wait_send()
        g_copy(h).wait_send()
        remote(sb.at[h], sb.at[h], tsend.at[h], trecv.at[h], partner).wait_send()
        for ring in (ring_y(h), ring_x(h), ring_x2(h), ring_y2(h)):
            ring.sent()
        remote(zr.at[h], zr.at[h], zsend.at[h], zrecv.at[h], partner).wait_send()
    remote(xp_v, xp_v, xsend.at[0], xrecv.at[0], partner).wait_send()


def shards(resp_q, resp_kv, resp_out_grad, resp_x, prompt_kv, stretch_offset):
    any_spec = pl.BlockSpec(memory_space=pl.ANY)
    vmem = pl.BlockSpec(memory_space=pltpu.VMEM)

    def ring_scratch(rows):
        return [
            pltpu.VMEM((KVH, RING, rows, PAIR), BF),
            pltpu.VMEM((KVH, 2, rows // 2, PAIR), BF),
            pltpu.VMEM((KVH, 2, rows, PAIR), BF),
        ]

    dma = pltpu.SemaphoreType.DMA
    return pl.pallas_call(
        kernel,
        out_shape=(
            jax.ShapeDtypeStruct((PLEN, KVW), F32),
            jax.ShapeDtypeStruct((32, KVW), F32),
        ),
        in_specs=[pl.BlockSpec(memory_space=pltpu.SMEM)] + [any_spec] * 5,
        out_specs=(vmem, vmem),
        scratch_shapes=[
            pltpu.VMEM((KVH, TOK, GROUP * HD), BF),
            pltpu.VMEM((KVH, TOK, GROUP * HD), BF),
            pltpu.VMEM((TOK, KVW), BF),
            pltpu.VMEM((TILES, TOK, HD), BF),
            pltpu.VMEM((TILES, TOK, HD), BF),
            pltpu.VMEM((TILES, HD, 2 * TOK), BF),
        ]
        + [pltpu.VMEM((5, 2, PLEN, HD), BF)] * KVH
        + [
            pltpu.VMEM((BLOCKS, PLEN, PAIR), F32),
            pltpu.VMEM((KVH, PLEN, PAIR), F32),
            pltpu.VMEM((KVH, 2 * TOK, PAIR), BF),
            pltpu.VMEM((KVH, 4, PLEN, PAIR), BF),
            pltpu.VMEM((KVH, 4, PLEN, PAIR), BF),
        ]
        + ring_scratch(ROWS_Y)
        + ring_scratch(ROWS_X)
        + ring_scratch(ROWS_Y // RING)
        + ring_scratch(ROWS_X // RING)
        + [
            pltpu.VMEM((KVH, RING, 32, PAIR), BF),
            pltpu.VMEM((KVH, 8, 32, PAIR), BF),
            dma((5, KVH)),
            dma((KVH,)), dma((KVH,)),
            dma((1,)), dma((1,)),
            dma((KVH,)), dma((KVH,)),
            dma((KVH,)), dma((KVH,)),
            dma((KVH,)), dma((KVH,)),
            dma((KVH, 4)), dma((KVH, 4, 4)),
        ],
        compiler_params=pltpu.CompilerParams(
            collective_id=0, has_side_effects=True, vmem_limit_bytes=56 * 1024 * 1024
        ),
        cost_estimate=pl.CostEstimate(
            flops=7_000_000_000, bytes_accessed=12_000_000, transcendentals=2_000_000
        ),
        name="attention_grads",
    )(stretch_offset, resp_q, resp_kv, resp_out_grad, resp_x, prompt_kv)


def solution(mesh):
    return jax.shard_map(
        shards,
        mesh=mesh,
        in_specs=(
            P(("cuts", "dev"), None),
            P(("cuts", "dev"), None),
            P(("cuts", "dev"), None),
            P(("cuts", "dev"), None),
            P(("cuts", "dev"), None),
            P(("cuts", "dev")),
        ),
        out_specs=(P(("cuts", "dev"), None), P("dev", None)),
        check_vma=False,
    )
```

```python
import math

import jax
import jax.numpy as jnp
from jax import lax
from jax.experimental import pallas as pl
from jax.experimental.pallas import tpu as pltpu
from jax.sharding import PartitionSpec as P

QH = 16
KVH = 4
GROUP = QH // KVH
HD = 128
PLEN = 128
STRETCH = 64
REACH = 2
KVW = 1024
HALF = KVH * HD
BLOCKS = 8
TOK = BLOCKS * STRETCH
RING = 4
TILES = 16
PAIR = 2 * HD
SPLIT = (((0, 1), (2, 3)),) * 4
SHIFT = (0, 1, 2, -1, -2)
SCALE = HD ** -0.5
LOG2E = 1.4426950408889634

BF = jnp.bfloat16
F32 = jnp.float32


def remote(src, dst, send, recv, device):
    return pltpu.make_async_remote_copy(
        src_ref=src,
        dst_ref=dst,
        send_sem=send,
        recv_sem=recv,
        device_id=device,
        device_id_type=pl.DeviceIdType.MESH,
    )


def nt(a, b):
    return lax.dot_general(a, b, (((1,), (1,)), ((), ())), preferred_element_type=F32)


def nn(a, b):
    return lax.dot_general(a, b, (((1,), (0,)), ((), ())), preferred_element_type=F32)


def place_of(x, core):
    same = (x // 2 + core + 1) % 2
    to_x = same * x + (1 - same) * (3 - x)
    to_core = same * (1 - core) + (1 - same) * core
    return to_x, to_core


def source_of(x, core):
    same = (x // 2 + core + 1) % 2
    from_x = (1 - same) * x + same * (3 - x)
    from_core = (1 - same) * (1 - core) + same * core
    return from_x, from_core


def part_of(x, core):
    to_x, to_core = place_of(x, core)
    return (to_x % 2) * 2 + to_core


class Ring:
    def __init__(self, refs, sems, mine, right, left, far, to_right, to_left):
        self.buf, self.near, self.full = refs
        self.recv, self.send = sems
        self.mine, self.right, self.left, self.far = mine, right, left, far
        self.to_right, self.to_left = to_right, to_left
        self.half = self.buf.shape[1] // 2

    def copy(self, which):
        low, high = pl.ds(0, self.half), pl.ds(self.half, self.half)
        source, target = (
            (self.buf.at[self.far, low], self.near.at[0]),
            (self.buf.at[self.far, high], self.near.at[1]),
            (self.buf.at[self.right, high], self.full.at[0, high]),
            (self.buf.at[self.left, low], self.full.at[1, low]),
            (self.buf.at[self.right, low], self.full.at[0, low]),
            (self.buf.at[self.left, high], self.full.at[1, high]),
        )[which]
        device = (self.to_right, self.to_left)[which % 2]
        return remote(source, target, self.send, self.recv.at[which], device)

    def start(self, *which):
        for one in which:
            self.copy(one).start()

    def second(self):
        half = self.half
        self.copy(0).wait_recv()
        self.buf[self.right, 0:half] = (
            self.buf[self.right, 0:half].astype(F32) + self.near[0].astype(F32)
        ).astype(BF)
        self.start(4)
        self.copy(1).wait_recv()
        self.buf[self.left, half:] = (
            self.buf[self.left, half:].astype(F32) + self.near[1].astype(F32)
        ).astype(BF)
        self.start(5)

    def arrive(self):
        for one in range(2, 6):
            self.copy(one).wait_recv()

    def total(self, rows):
        return (
            self.buf[self.mine, rows].astype(F32)
            + self.full[0, rows].astype(F32)
            + self.full[1, rows].astype(F32)
        )

    def sent(self):
        whole = self.buf.at[pl.ds(0, 3)]
        remote(whole, whole, self.send, self.recv.at[0], self.to_right).wait_send()


class Direct:
    def __init__(self, refs, sems, mine, chunks, devices):
        self.buf, self.full = refs
        self.recv, self.send = sems
        self.mine, self.chunks, self.devices = mine, chunks, devices

    def first(self):
        for step in range(3):
            remote(
                self.buf.at[self.chunks[step]], self.full.at[step], self.send, self.recv.at[0],
                self.devices[step],
            ).start()

    def arrive(self):
        remote(self.full, self.full, self.send, self.recv.at[0], self.devices[0]).wait_recv()

    def total(self, rows):
        done = self.buf[self.mine, rows].astype(F32)
        for step in range(3):
            done = done + self.full[step, rows].astype(F32)
        return done

    def sent(self):
        remote(self.full, self.full, self.send, self.recv.at[0], self.devices[0]).wait_send()


def kernel(
    off_ref, q_hbm, kv_hbm, do_hbm, x_hbm, p_hbm, outp_ref, outw_ref,
    q_v, do_v, kv_v, xo_v, xp_v, xt_v, pk0, pk1, pk2, pk3, tb, po, g_v, sb, rb, cb,
    zs, zr, load_sem, psend, precv, xsend, xrecv, gsend, grecv, tsend, trecv, zsend, zrecv,
    rsend, rrecv, *rings,
):
    cut = lax.axis_index("cuts")
    dev = lax.axis_index("dev")
    count = lax.axis_size("dev")
    core = dev % 2
    x = (dev // 2) % RING
    zh = (dev // 8) % RING
    y = dev // 32
    pk = (pk0, pk1, pk2, pk3)

    def at(y_, zh_, x_, core_):
        return ((y_ * RING + zh_) * RING + x_) * 2 + core_

    partner = (cut, at(y, zh, x, 1 - core))
    x_far, y_far = (cut, at(y, zh, (x + 2) % RING, core)), (cut, at((y + 2) % RING, zh, x, core))
    x_right, x_left = (cut, at(y, zh, (x + 1) % RING, core)), (cut, at(y, zh, (x + 3) % RING, core))
    y_right, y_left = (cut, at((y + 1) % RING, zh, x, core)), (cut, at((y + 3) % RING, zh, x, core))
    ahead, behind = (cut, (dev + 2) % count), (cut, (dev + count - 2) % count)
    to_x, to_core = place_of(x, core)
    from_x, from_core = source_of(x, core)

    def own_loads(h):
        cols = pl.ds(h * GROUP * HD, GROUP * HD)
        return (
            pltpu.make_async_copy(q_hbm.at[:, cols], q_v.at[h], load_sem.at[0, h]),
            pltpu.make_async_copy(do_hbm.at[:, cols], do_v.at[h], load_sem.at[1, h]),
        )

    def prompt_loads(h):
        return (
            pltpu.make_async_copy(
                p_hbm.at[:, pl.ds(h * HD, HD)], pk[h].at[0, 0], load_sem.at[2, h]
            ),
            pltpu.make_async_copy(
                p_hbm.at[:, pl.ds(HALF + h * HD, HD)], pk[h].at[0, 1], load_sem.at[3, h]
            ),
        )

    kv_load = pltpu.make_async_copy(kv_hbm, kv_v, load_sem.at[4, 0])

    @pl.loop(0, TILES)
    def _(t):
        cols = pl.ds(pl.multiple_of((t * 2 + core) * HD, HD), HD)
        pltpu.make_async_copy(x_hbm.at[:, cols], xo_v.at[t], load_sem.at[4, 1]).start()

    for h in range(KVH):
        for copy in prompt_loads(h) + own_loads(h):
            copy.start()
        if h == 0:
            kv_load.start()

    barrier = pltpu.get_barrier_semaphore()

    def greet(device):
        pl.semaphore_signal(
            barrier, inc=1, device_id=device, device_id_type=pl.DeviceIdType.MESH
        )

    for device in (partner, ahead, behind, x_right, x_left, x_far, y_right, y_left, y_far):
        greet(device)
    for zl_ in range(2):
        for zh_ in range(RING):
            greet((zl_, at(y, zh_, from_x, from_core)))

    pl.semaphore_wait(barrier, 9 + 8)

    def prompt_copies(h, slot, device, send, recv):
        return [
            remote(
                p_hbm.at[:, pl.ds(part * HALF + h * HD, HD)], pk[h].at[slot, part],
                psend.at[h, send], precv.at[h, recv], device,
            )
            for part in range(2)
        ]

    def send_far(h):
        for copy in prompt_copies(h, 2, ahead, 0, 0) + prompt_copies(h, 4, behind, 0, 1):
            copy.start()

    def send_partner(h):
        for copy in prompt_copies(h, 1 + 2 * core, partner, 1, 2):
            copy.start()

    def pass_copy(h):
        return remote(
            pk[h].at[4 - 2 * core], pk[h].at[3 - 2 * core], psend.at[h, 2], precv.at[h, 3], partner
        )

    def slot_copy(h, slot, send, recv):
        return remote(pk[h].at[slot], pk[h].at[slot], psend.at[h, send], precv.at[h, recv], partner)

    def relay(h):
        slot_copy(h, 2, 0, 0).wait_recv()
        slot_copy(h, 4, 0, 1).wait_recv()
        pass_copy(h).start()

    send_far(0)
    for h in range(KVH):
        send_partner(h)
    send_far(1)

    @pl.loop(0, TILES)
    def _(t):
        cols = pl.ds(pl.multiple_of((t * 2 + 1 - core) * HD, HD), HD)
        remote(x_hbm.at[:, cols], xp_v.at[t], xsend.at[0], xrecv.at[0], partner).start()

    pltpu.make_async_copy(xo_v, xo_v, load_sem.at[4, 1]).wait()

    @pl.loop(0, TILES)
    def _(t):
        xt_v[t, :, 0:TOK] = xo_v[t].T

    key_at = lax.broadcasted_iota(jnp.int32, (STRETCH, GROUP * STRETCH), 0)
    query_at = lax.broadcasted_iota(jnp.int32, (STRETCH, GROUP * STRETCH), 1) % STRETCH
    seen = key_at <= query_at

    def slot_of(c):
        off = off_ref[c]
        return jnp.where(off >= 0, off, REACH - off)

    def block(h, c):
        slot = slot_of(c)
        rows = pl.ds(pl.multiple_of(c * STRETCH, STRETCH), STRETCH)
        queries = jnp.concatenate(
            [q_v[h, rows, g * HD:(g + 1) * HD] for g in range(GROUP)], axis=0
        )
        dout = jnp.concatenate(
            [do_v[h, rows, g * HD:(g + 1) * HD] for g in range(GROUP)], axis=0
        )
        keys = jnp.concatenate([pk[h][slot, 0], kv_v[rows, h * HD:(h + 1) * HD]], axis=0)
        values = jnp.concatenate(
            [pk[h][slot, 1], kv_v[rows, HALF + h * HD:HALF + (h + 1) * HD]], axis=0
        )
        scores = nt(keys, queries)
        dprobs = nt(values, dout)
        scores = jnp.concatenate(
            [scores[:PLEN], jnp.where(seen, scores[PLEN:], -1e30)], axis=0
        )
        top = jnp.max(scores, axis=0, keepdims=True)
        expo = jnp.exp2((scores - top) * (SCALE * LOG2E))
        probs = expo * (1.0 / jnp.sum(expo, axis=0, keepdims=True))
        probs_b = probs.astype(BF)
        rowdot = jnp.sum(probs_b.astype(F32) * dprobs, axis=0, keepdims=True)
        dscores_b = (probs * (dprobs - rowdot)).astype(BF)
        kgrad = nn(dscores_b, queries) * SCALE
        vgrad = nn(probs_b, dout)
        g_v[h, rows, 0:HD] = kgrad[PLEN:].astype(BF)
        g_v[h, rows, HD:] = vgrad[PLEN:].astype(BF)
        tb[c, :, 0:HD] = kgrad[:PLEN]
        tb[c, :, HD:] = vgrad[:PLEN]

    def g_copy(h):
        return remote(
            g_v.at[h, pl.ds(0, TOK)], g_v.at[h, pl.ds(TOK, TOK)], gsend.at[h], grecv.at[h], partner
        )

    def term_copies(h):
        to_ahead = remote(sb.at[h, 3], rb.at[h, 2], tsend.at[h, 0], trecv.at[h, 2], ahead)
        to_behind = remote(sb.at[h, 1], rb.at[h, 1], tsend.at[h, 1], trecv.at[h, 1], behind)
        return to_ahead, to_behind

    def partner_terms(h):
        return (
            remote(sb.at[h, 2 * core], cb.at[h], tsend.at[h, 2], trecv.at[h, 3], partner),
            remote(sb.at[h, 2 - 2 * core], rb.at[h, 0], tsend.at[h, 3], trecv.at[h, 0], partner),
        )

    def back(h):
        partner_terms(h)[0].wait_recv()
        slot = 3 - 2 * core

        @pl.loop(0, PLEN // 32)
        def _(i):
            rows = pl.ds(pl.multiple_of(i * 32, 32), 32)
            sb[h, slot, rows] = (sb[h, slot, rows].astype(F32) + cb[h, rows].astype(F32)).astype(BF)

        for copy in term_copies(h):
            copy.start()

    def ready(h):
        for copy in prompt_loads(h) + own_loads(h):
            copy.wait()
        if h == 0:
            kv_load.wait()
        slot_copy(h, 1 + 2 * core, 1, 2).wait_recv()
        slot_copy(h, 3 - 2 * core, 2, 3).wait_recv()

    def attend(h, half):
        @pl.loop(half * 2, half * 2 + 2)
        def _(i):
            block(h, i * 2)
            block(h, i * 2 + 1)

    def combine(h):

        slots = [slot_of(c) for c in range(BLOCKS)]

        @pl.loop(0, PLEN // 16)
        def _(i):
            rows = pl.ds(pl.multiple_of(i * 16, 16), 16)
            sums = [jnp.zeros((16, PAIR), F32) for _ in SHIFT]
            for c in range(BLOCKS):
                term = tb[c, rows]
                for n in range(len(SHIFT)):
                    sums[n] = sums[n] + jnp.where(slots[c] == n, term, 0.0)
            po[h, rows] = sums[0]
            for n in range(1, len(SHIFT)):
                sb[h, n - 1, rows] = sums[n].astype(BF)

        for copy in partner_terms(h):
            copy.start()

    y_at = [(y + step) % RING for step in range(RING)]
    x_at = [part_of((x + step) % RING, core) for step in range(RING)]

    def sems(h, which):
        return rrecv.at[h, which], rsend.at[h, which]

    def ring_y(h):
        return Ring(
            rings[h * 10:h * 10 + 3], sems(h, 0), y_at[0], y_at[1], y_at[3], y_at[2], y_right, y_left
        )

    def ring_x(h):
        return Ring(
            rings[h * 10 + 3:h * 10 + 6], sems(h, 1), x_at[0], x_at[1], x_at[3], x_at[2],
            x_right, x_left,
        )

    def then_x(h):
        return Direct(
            rings[h * 10 + 6:h * 10 + 8], sems(h, 2), x_at[0],
            (x_at[2], x_at[1], x_at[3]), (x_far, x_right, x_left),
        )

    def then_y(h):
        return Direct(
            rings[h * 10 + 8:h * 10 + 10], sems(h, 3), y_at[0],
            (y_at[2], y_at[1], y_at[3]), (y_far, y_right, y_left),
        )

    def product(h):
        g_copy(h).wait_recv()
        over_y, over_x = ring_y(h), ring_x(h)

        def chunk(step):
            to = (y + 2 + step) % RING
            left = xt_v[pl.ds(to * RING, RING)].reshape(RING * 128, 2 * TOK)
            out = nn(left, g_v[h]).astype(BF)
            for place, z in enumerate(SPLIT[h][0]):
                over_y.buf[to, place * 128:(place + 1) * 128] = out[z * 128:(z + 1) * 128]
            rows = len(SPLIT[h][1]) * 32
            for place, z in enumerate(SPLIT[h][1]):
                for k in range(RING):
                    row = pl.multiple_of(to * rows + place * 32, 32)
                    over_x.buf[k, pl.ds(row, 32)] = out[z * 128 + k * 32:z * 128 + (k + 1) * 32]

        chunk(0)
        over_y.start(0, 1)

        @pl.loop(1, RING)
        def _(step):
            chunk(step)

        over_x.start(0, 1)
        over_y.start(2, 3)
        over_x.start(2, 3)

    def second(h):
        ring_y(h).second()
        ring_x(h).second()

    def third(h):
        ring, then = ring_y(h), then_x(h)
        ring.arrive()
        for place in range(len(SPLIT[h][0])):
            for k in range(RING):
                row = place * 128 + k * 32
                then.buf[k, place * 32:(place + 1) * 32] = ring.total(pl.ds(row, 32)).astype(BF)
        then.first()
        ring, then = ring_x(h), then_y(h)
        ring.arrive()
        rows = len(SPLIT[h][1]) * 32
        for k in range(RING):
            then.buf[k] = ring.total(pl.ds(k * rows, rows)).astype(BF)
        then.first()

    def z_copy(h, zl_, zh_):
        return remote(
            zs.at[h, zh_], zr.at[h, zh * 2 + cut], zsend.at[h], zrecv.at[h],
            (zl_, at(y, zh_, to_x, to_core)),
        )

    def fourth(h):
        ring = then_x(h)
        ring.arrive()
        for place, z in enumerate(SPLIT[h][0]):
            zs[h, z] = ring.total(pl.ds(place * 32, 32)).astype(BF)
        ring = then_y(h)
        ring.arrive()
        for place, z in enumerate(SPLIT[h][1]):
            zs[h, z] = ring.total(pl.ds(place * 32, 32)).astype(BF)
        for zh_ in range(RING):
            for zl_ in range(2):
                z_copy(h, zl_, zh_).start()

    def last(h):
        remote(zr.at[h], zr.at[h], zsend.at[h], zrecv.at[h], partner).wait_recv()
        done = zr[h, 0].astype(F32)
        for source in range(1, 8):
            done = done + zr[h, source].astype(F32)
        outw_ref[:, h * HD:(h + 1) * HD] = done[:, :HD]
        outw_ref[:, HALF + h * HD:HALF + (h + 1) * HD] = done[:, HD:]

    def prompt_last(h):
        partner_terms(h)[1].wait_recv()
        for n in (1, 2):
            remote(rb.at[h, n], rb.at[h, n], tsend.at[h, 0], trecv.at[h, n], partner).wait_recv()

        @pl.loop(0, PLEN // 32)
        def _(i):
            rows = pl.ds(pl.multiple_of(i * 32, 32), 32)
            done = po[h, rows]
            for n in range(3):
                done = done + rb[h, n, rows].astype(F32)
            outp_ref[rows, h * HD:(h + 1) * HD] = done[:, :HD]
            outp_ref[rows, HALF + h * HD:HALF + (h + 1) * HD] = done[:, HD:]

    relay(0)
    send_far(2)
    ready(0)
    attend(0, 0)
    attend(0, 1)
    g_copy(0).start()
    relay(1)
    send_far(3)
    combine(0)
    remote(xp_v, xp_v, xsend.at[0], xrecv.at[0], partner).wait_recv()

    @pl.loop(0, TILES)
    def _(t):
        xt_v[t, :, TOK:] = xp_v[t].T

    product(0)
    back(0)
    ready(1)
    attend(1, 0)
    relay(2)
    attend(1, 1)
    g_copy(1).start()
    second(0)
    combine(1)
    product(1)
    back(1)
    ready(2)
    attend(2, 0)
    third(0)
    relay(3)
    attend(2, 1)
    g_copy(2).start()
    second(1)
    combine(2)
    product(2)
    back(2)
    fourth(0)
    ready(3)
    attend(3, 0)
    third(1)
    attend(3, 1)
    g_copy(3).start()
    second(2)
    combine(3)
    product(3)
    fourth(1)
    back(3)
    third(2)
    second(3)
    fourth(2)
    prompt_last(0)
    third(3)
    prompt_last(1)
    fourth(3)
    prompt_last(2)
    last(0)
    last(1)
    prompt_last(3)
    last(2)
    last(3)

    for h in range(KVH):
        far = pk[h].at[pl.ds(0, 2)]
        remote(far, far, psend.at[h, 0], precv.at[h, 0], partner).wait_send()
        slot_copy(h, 1, 1, 2).wait_send()
        pass_copy(h).wait_send()
        g_copy(h).wait_send()
        for copy in term_copies(h) + partner_terms(h):
            copy.wait_send()
        for ring in (ring_y(h), ring_x(h), then_x(h), then_y(h)):
            ring.sent()
        remote(zr.at[h], zr.at[h], zsend.at[h], zrecv.at[h], partner).wait_send()
    remote(xp_v, xp_v, xsend.at[0], xrecv.at[0], partner).wait_send()


def hand_on(prompt_ref, weight_ref, outp_ref, outw_ref):
    outp_ref[...] = prompt_ref[...]
    outw_ref[...] = weight_ref[...]


def shards(resp_q, resp_kv, resp_out_grad, resp_x, prompt_kv, stretch_offset):
    any_spec = pl.BlockSpec(memory_space=pl.ANY)
    vmem = pl.BlockSpec(memory_space=pltpu.VMEM)

    def buffers(*shapes):
        return [pltpu.VMEM(shape + (PAIR,), BF) for shape in shapes]

    rings = []
    for first_y, first_x in SPLIT:
        for parts in (len(first_y), len(first_x)):
            rings += buffers((RING, parts * 128), (2, parts * 64), (2, parts * 128))
        for parts in (len(first_y), len(first_x)):
            rings += buffers((RING, parts * 32), (3, parts * 32))

    dma = pltpu.SemaphoreType.DMA
    grads = pl.pallas_call(
        kernel,
        out_shape=(
            jax.ShapeDtypeStruct((PLEN, KVW), F32),
            jax.ShapeDtypeStruct((32, KVW), F32),
        ),
        in_specs=[pl.BlockSpec(memory_space=pltpu.SMEM)] + [any_spec] * 5,
        out_specs=(vmem, vmem),
        scratch_shapes=[
            pltpu.VMEM((KVH, TOK, GROUP * HD), BF),
            pltpu.VMEM((KVH, TOK, GROUP * HD), BF),
            pltpu.VMEM((TOK, KVW), BF),
            pltpu.VMEM((TILES, TOK, HD), BF),
            pltpu.VMEM((TILES, TOK, HD), BF),
            pltpu.VMEM((TILES, HD, 2 * TOK), BF),
        ]
        + [pltpu.VMEM((5, 2, PLEN, HD), BF)] * KVH
        + [
            pltpu.VMEM((BLOCKS, PLEN, PAIR), F32),
            pltpu.VMEM((KVH, PLEN, PAIR), F32),
            pltpu.VMEM((KVH, 2 * TOK, PAIR), BF),
            pltpu.VMEM((KVH, 4, PLEN, PAIR), BF),
            pltpu.VMEM((KVH, 3, PLEN, PAIR), BF),
            pltpu.VMEM((KVH, PLEN, PAIR), BF),
        ]
        + [
            pltpu.VMEM((KVH, RING, 32, PAIR), BF),
            pltpu.VMEM((KVH, 8, 32, PAIR), BF),
            dma((5, KVH)),
            dma((KVH, 3)), dma((KVH, 4)),
            dma((1,)), dma((1,)),
            dma((KVH,)), dma((KVH,)),
            dma((KVH, 4)), dma((KVH, 4)),
            dma((KVH,)), dma((KVH,)),
            dma((KVH, 4)), dma((KVH, 4, 6)),
        ]
        + rings,
        compiler_params=pltpu.CompilerParams(
            collective_id=0, has_side_effects=True, vmem_limit_bytes=56 * 1024 * 1024
        ),
        cost_estimate=pl.CostEstimate(
            flops=7_000_000_000, bytes_accessed=12_000_000, transcendentals=2_000_000
        ),
        name="attention_grads",
    )(stretch_offset, resp_q, resp_kv, resp_out_grad, resp_x, prompt_kv)
    return pl.pallas_call(
        hand_on,
        out_shape=(
            jax.ShapeDtypeStruct((PLEN, KVW), F32),
            jax.ShapeDtypeStruct((32, KVW), F32),
        ),
        in_specs=[vmem, vmem],
        out_specs=(vmem, vmem),
        name="hand_on",
    )(*grads)


def solution(mesh):
    return jax.shard_map(
        shards,
        mesh=mesh,
        in_specs=(
            P(("cuts", "dev"), None),
            P(("cuts", "dev"), None),
            P(("cuts", "dev"), None),
            P(("cuts", "dev"), None),
            P(("cuts", "dev"), None),
            P(("cuts", "dev")),
        ),
        out_specs=(P(("cuts", "dev"), None), P("dev", None)),
        check_vma=False,
    )
```

```python
import math

import jax
import jax.numpy as jnp
from jax import lax
from jax.experimental import pallas as pl
from jax.experimental.pallas import tpu as pltpu
from jax.sharding import PartitionSpec as P

QH = 16
KVH = 4
GROUP = QH // KVH
HD = 128
PLEN = 128
STRETCH = 64
REACH = 2
KVW = 1024
HALF = KVH * HD
BLOCKS = 8
TOK = BLOCKS * STRETCH
RING = 4
TILES = 16
PAIR = 2 * HD
FIRST_Y = (0, 1)
FIRST_X = (2, 3)
SHIFT = (0, 1, 2, -1, -2)
SCALE = HD ** -0.5
LOG2E = 1.4426950408889634

BF = jnp.bfloat16
F32 = jnp.float32


def remote(src, dst, send, recv, device):
    return pltpu.make_async_remote_copy(
        src_ref=src,
        dst_ref=dst,
        send_sem=send,
        recv_sem=recv,
        device_id=device,
        device_id_type=pl.DeviceIdType.MESH,
    )


def nt(a, b):
    return lax.dot_general(a, b, (((1,), (1,)), ((), ())), preferred_element_type=F32)


def nn(a, b):
    return lax.dot_general(a, b, (((1,), (0,)), ((), ())), preferred_element_type=F32)


def place_of(x, core):
    same = (x // 2 + core + 1) % 2
    to_x = same * x + (1 - same) * (3 - x)
    to_core = same * (1 - core) + (1 - same) * core
    return to_x, to_core


def source_of(x, core):
    same = (x // 2 + core + 1) % 2
    from_x = (1 - same) * x + same * (3 - x)
    from_core = (1 - same) * (1 - core) + same * core
    return from_x, from_core


def part_of(x, core):
    to_x, to_core = place_of(x, core)
    return (to_x % 2) * 2 + to_core


class Ring:
    def __init__(self, refs, sems, mine, right, left, far, to_right, to_left):
        self.buf, self.near, self.full = refs
        self.recv, self.send = sems
        self.mine, self.right, self.left, self.far = mine, right, left, far
        self.to_right, self.to_left = to_right, to_left
        self.half = self.buf.shape[1] // 2

    def copy(self, which):
        low, high = pl.ds(0, self.half), pl.ds(self.half, self.half)
        source, target = (
            (self.buf.at[self.far, low], self.near.at[0]),
            (self.buf.at[self.far, high], self.near.at[1]),
            (self.buf.at[self.right, high], self.full.at[0, high]),
            (self.buf.at[self.left, low], self.full.at[1, low]),
            (self.buf.at[self.right, low], self.full.at[0, low]),
            (self.buf.at[self.left, high], self.full.at[1, high]),
        )[which]
        device = (self.to_right, self.to_left)[which % 2]
        return remote(source, target, self.send, self.recv.at[which], device)

    def start(self, *which):
        for one in which:
            self.copy(one).start()

    def second(self):
        half = self.half
        self.copy(0).wait_recv()
        self.buf[self.right, 0:half] = (
            self.buf[self.right, 0:half].astype(F32) + self.near[0].astype(F32)
        ).astype(BF)
        self.start(4)
        self.copy(1).wait_recv()
        self.buf[self.left, half:] = (
            self.buf[self.left, half:].astype(F32) + self.near[1].astype(F32)
        ).astype(BF)
        self.start(5)

    def arrive(self):
        for one in range(2, 6):
            self.copy(one).wait_recv()

    def total(self, rows):
        return (
            self.buf[self.mine, rows].astype(F32)
            + self.full[0, rows].astype(F32)
            + self.full[1, rows].astype(F32)
        )

    def sent(self):
        whole = self.buf.at[pl.ds(0, 3)]
        remote(whole, whole, self.send, self.recv.at[0], self.to_right).wait_send()


class Direct:
    def __init__(self, refs, sems, mine, chunks, devices):
        self.buf, self.full = refs
        self.recv, self.send = sems
        self.mine, self.chunks, self.devices = mine, chunks, devices

    def first(self):
        for step in range(3):
            remote(
                self.buf.at[self.chunks[step]], self.full.at[step], self.send, self.recv.at[0],
                self.devices[step],
            ).start()

    def arrive(self):
        remote(self.full, self.full, self.send, self.recv.at[0], self.devices[0]).wait_recv()

    def total(self, rows):
        done = self.buf[self.mine, rows].astype(F32)
        for step in range(3):
            done = done + self.full[step, rows].astype(F32)
        return done

    def sent(self):
        remote(self.full, self.full, self.send, self.recv.at[0], self.devices[0]).wait_send()


def kernel(
    off_ref, q_hbm, kv_hbm, do_hbm, x_hbm, p_hbm, outp_ref, outw_ref,
    q_v, do_v, kv_v, xo_v, xp_v, xt_v, pk, tb, po, g_v, sb, rb, cb,
    zs, zr, load_sem, psend, precv, xsend, xrecv, gsend, grecv, tsend, trecv, zsend, zrecv,
    rsend, rrecv, *rings,
):
    cut = lax.axis_index("cuts")
    dev = lax.axis_index("dev")
    count = lax.axis_size("dev")
    core = dev % 2
    x = (dev // 2) % RING
    zh = (dev // 8) % RING
    y = dev // 32

    def at(y_, zh_, x_, core_):
        return ((y_ * RING + zh_) * RING + x_) * 2 + core_

    partner = (cut, at(y, zh, x, 1 - core))
    x_far, y_far = (cut, at(y, zh, (x + 2) % RING, core)), (cut, at((y + 2) % RING, zh, x, core))
    x_right, x_left = (cut, at(y, zh, (x + 1) % RING, core)), (cut, at(y, zh, (x + 3) % RING, core))
    y_right, y_left = (cut, at((y + 1) % RING, zh, x, core)), (cut, at((y + 3) % RING, zh, x, core))
    ahead, behind = (cut, (dev + 2) % count), (cut, (dev + count - 2) % count)
    to_x, to_core = place_of(x, core)
    from_x, from_core = source_of(x, core)

    barrier = pltpu.get_barrier_semaphore()

    def greet(device):
        pl.semaphore_signal(
            barrier, inc=1, device_id=device, device_id_type=pl.DeviceIdType.MESH
        )

    for step in (2, 1, 3, 0):
        for zl_ in range(2):
            greet((zl_, at(y, (zh + step) % RING, from_x, from_core)))
    for device in (partner, ahead, behind, x_right, x_left, x_far, y_right, y_left, y_far):
        greet(device)
    def cols_of(h, part=0):
        return pl.ds(pl.multiple_of(part * HALF + h * HD, HD), HD)

    def own_loads(h):
        cols = pl.ds(pl.multiple_of(h * GROUP * HD, GROUP * HD), GROUP * HD)
        return (
            pltpu.make_async_copy(q_hbm.at[:, cols], q_v.at[h], load_sem.at[0, h]),
            pltpu.make_async_copy(do_hbm.at[:, cols], do_v.at[h], load_sem.at[1, h]),
        )

    def prompt_loads(h):
        return (
            pltpu.make_async_copy(
                p_hbm.at[:, cols_of(h)], pk.at[h, 0, 0], load_sem.at[2, h]
            ),
            pltpu.make_async_copy(
                p_hbm.at[:, cols_of(h, 1)], pk.at[h, 0, 1], load_sem.at[3, h]
            ),
        )

    kv_load = pltpu.make_async_copy(kv_hbm, kv_v, load_sem.at[4, 0])

    kv_load.start()

    @pl.loop(0, KVH)
    def _(h):
        for copy in prompt_loads(h) + own_loads(h):
            copy.start()

    pl.semaphore_wait(barrier, 9 + 8)

    def prompt_copies(h, slot, device, send, recv):
        return [
            remote(
                p_hbm.at[:, cols_of(h, part)], pk.at[h, slot, part],
                psend.at[h, send], precv.at[h, recv], device,
            )
            for part in range(2)
        ]

    def send_far(h):
        for copy in prompt_copies(h, 2, ahead, 0, 0) + prompt_copies(h, 4, behind, 0, 1):
            copy.start()

    def send_partner(h):
        for copy in prompt_copies(h, 1 + 2 * core, partner, 1, 2):
            copy.start()

    def pass_copy(h):
        return remote(
            pk.at[h, 4 - 2 * core], pk.at[h, 3 - 2 * core], psend.at[h, 2], precv.at[h, 3], partner
        )

    def slot_copy(h, slot, send, recv):
        return remote(pk.at[h, slot], pk.at[h, slot], psend.at[h, send], precv.at[h, recv], partner)

    def relay(h):
        slot_copy(h, 2, 0, 0).wait_recv()
        slot_copy(h, 4, 0, 1).wait_recv()
        pass_copy(h).start()

    @pl.loop(0, KVH)
    def _(h):
        send_far(h)
        send_partner(h)

    @pl.loop(0, TILES)
    def _(t):
        cols = pl.ds(pl.multiple_of((t * 2 + core) * HD, HD), HD)
        pltpu.make_async_copy(x_hbm.at[:, cols], xo_v.at[t], load_sem.at[4, 1]).start()

    @pl.loop(0, TILES)
    def _(t):
        cols = pl.ds(pl.multiple_of((t * 2 + 1 - core) * HD, HD), HD)
        remote(x_hbm.at[:, cols], xp_v.at[t], xsend.at[0], xrecv.at[0], partner).start()

    pltpu.make_async_copy(xo_v, xo_v, load_sem.at[4, 1]).wait()

    @pl.loop(0, TILES)
    def _(t):
        xt_v[t, :, 0:TOK] = xo_v[t].T

    key_at = lax.broadcasted_iota(jnp.int32, (STRETCH, GROUP * STRETCH), 0)
    query_at = lax.broadcasted_iota(jnp.int32, (STRETCH, GROUP * STRETCH), 1) % STRETCH
    seen = key_at <= query_at

    def slot_of(c):
        off = off_ref[c]
        return jnp.where(off >= 0, off, REACH - off)

    def block(h, c):
        slot = slot_of(c)
        rows = pl.ds(pl.multiple_of(c * STRETCH, STRETCH), STRETCH)
        queries = jnp.concatenate(
            [q_v[h, rows, g * HD:(g + 1) * HD] for g in range(GROUP)], axis=0
        )
        dout = jnp.concatenate(
            [do_v[h, rows, g * HD:(g + 1) * HD] for g in range(GROUP)], axis=0
        )
        prompt = [pk[h, 0, part] for part in range(2)]
        for n in range(1, len(SHIFT)):
            prompt = [jnp.where(slot == n, pk[h, n, part], prompt[part]) for part in range(2)]
        keys, values = [
            jnp.concatenate([prompt[part], kv_v[rows, cols_of(h, part)]], axis=0)
            for part in range(2)
        ]
        scores = nt(keys, queries)
        dprobs = nt(values, dout)
        scores = jnp.concatenate(
            [scores[:PLEN], jnp.where(seen, scores[PLEN:], -1e30)], axis=0
        )
        top = jnp.max(scores, axis=0, keepdims=True)
        expo = jnp.exp2((scores - top) * (SCALE * LOG2E))
        probs = expo * (1.0 / jnp.sum(expo, axis=0, keepdims=True))
        probs_b = probs.astype(BF)
        rowdot = jnp.sum(probs_b.astype(F32) * dprobs, axis=0, keepdims=True)
        dscores_b = (probs * (dprobs - rowdot)).astype(BF)
        kgrad = nn(dscores_b, queries) * SCALE
        vgrad = nn(probs_b, dout)
        g_v[h, rows, 0:HD] = kgrad[PLEN:].astype(BF)
        g_v[h, rows, HD:] = vgrad[PLEN:].astype(BF)
        tb[c, :, 0:HD] = kgrad[:PLEN]
        tb[c, :, HD:] = vgrad[:PLEN]

    def g_copy(h):
        return remote(
            g_v.at[h, pl.ds(0, TOK)], g_v.at[h, pl.ds(TOK, TOK)], gsend.at[h], grecv.at[h], partner
        )

    def term_copies(h):
        to_ahead = remote(sb.at[h, 3], rb.at[h, 2], tsend.at[h, 0], trecv.at[h, 2], ahead)
        to_behind = remote(sb.at[h, 1], rb.at[h, 1], tsend.at[h, 1], trecv.at[h, 1], behind)
        return to_ahead, to_behind

    def partner_terms(h):
        return (
            remote(sb.at[h, 2 * core], cb.at[h], tsend.at[h, 2], trecv.at[h, 3], partner),
            remote(sb.at[h, 2 - 2 * core], rb.at[h, 0], tsend.at[h, 3], trecv.at[h, 0], partner),
        )

    def back(h):
        partner_terms(h)[0].wait_recv()
        slot = 3 - 2 * core

        @pl.loop(0, PLEN // 32)
        def _(i):
            rows = pl.ds(pl.multiple_of(i * 32, 32), 32)
            sb[h, slot, rows] = (sb[h, slot, rows].astype(F32) + cb[h, rows].astype(F32)).astype(BF)

        for copy in term_copies(h):
            copy.start()

    def ready(h):
        for copy in prompt_loads(h) + own_loads(h):
            copy.wait()
        slot_copy(h, 1 + 2 * core, 1, 2).wait_recv()
        slot_copy(h, 3 - 2 * core, 2, 3).wait_recv()

    def combine(h):

        slots = [slot_of(c) for c in range(BLOCKS)]

        @pl.loop(0, PLEN // 16)
        def _(i):
            rows = pl.ds(pl.multiple_of(i * 16, 16), 16)
            sums = [jnp.zeros((16, PAIR), F32) for _ in SHIFT]
            for c in range(BLOCKS):
                term = tb[c, rows]
                for n in range(len(SHIFT)):
                    sums[n] = sums[n] + jnp.where(slots[c] == n, term, 0.0)
            po[h, rows] = sums[0]
            for n in range(1, len(SHIFT)):
                sb[h, n - 1, rows] = sums[n].astype(BF)

        for copy in partner_terms(h):
            copy.start()

    y_at = [(y + step) % RING for step in range(RING)]
    x_at = [part_of((x + step) % RING, core) for step in range(RING)]

    def head(h, first, end):
        return [ref.at[h] for ref in rings[first:end]]

    def sems(h, which):
        return rrecv.at[h, which], rsend.at[h, which]

    def ring_y(h):
        return Ring(
            head(h, 0, 3), sems(h, 0), y_at[0], y_at[1], y_at[3], y_at[2], y_right, y_left
        )

    def ring_x(h):
        return Ring(
            head(h, 3, 6), sems(h, 1), x_at[0], x_at[1], x_at[3], x_at[2],
            x_right, x_left,
        )

    def then_x(h):
        return Direct(
            head(h, 6, 8), sems(h, 2), x_at[0],
            (x_at[2], x_at[1], x_at[3]), (x_far, x_right, x_left),
        )

    def then_y(h):
        return Direct(
            head(h, 8, 10), sems(h, 3), y_at[0],
            (y_at[2], y_at[1], y_at[3]), (y_far, y_right, y_left),
        )

    def product(h):
        g_copy(h).wait_recv()
        over_y, over_x = ring_y(h), ring_x(h)

        def chunk(step):
            to = (y + 2 + step) % RING
            left = xt_v[pl.ds(to * RING, RING)].reshape(RING * 128, 2 * TOK)
            out = nn(left, g_v[h]).astype(BF)
            for place, z in enumerate(FIRST_Y):
                over_y.buf[to, place * 128:(place + 1) * 128] = out[z * 128:(z + 1) * 128]
            rows = len(FIRST_X) * 32
            for place, z in enumerate(FIRST_X):
                for k in range(RING):
                    row = pl.multiple_of(to * rows + place * 32, 32)
                    over_x.buf[k, pl.ds(row, 32)] = out[z * 128 + k * 32:z * 128 + (k + 1) * 32]

        @pl.loop(0, RING)
        def _(step):
            chunk(step)

            @pl.when(step == 0)
            def _():
                over_y.start(0, 1)

        over_x.start(0, 1)
        over_y.start(2, 3)
        over_x.start(2, 3)

    def second(h):
        ring_y(h).second()
        ring_x(h).second()

    def third(h):
        ring, then = ring_y(h), then_x(h)
        ring.arrive()
        for place in range(len(FIRST_Y)):
            for k in range(RING):
                row = place * 128 + k * 32
                then.buf[k, place * 32:(place + 1) * 32] = ring.total(pl.ds(row, 32)).astype(BF)
        then.first()
        ring, then = ring_x(h), then_y(h)
        ring.arrive()
        rows = len(FIRST_X) * 32
        for k in range(RING):
            then.buf[k] = ring.total(pl.ds(k * rows, rows)).astype(BF)
        then.first()

    def z_copy(h, zl_, zh_):
        return remote(
            zs.at[h, zh_], zr.at[h, zh * 2 + cut], zsend.at[h], zrecv.at[h],
            (zl_, at(y, zh_, to_x, to_core)),
        )

    def fourth(h):
        ring = then_x(h)
        ring.arrive()
        for place, z in enumerate(FIRST_Y):
            zs[h, z] = ring.total(pl.ds(place * 32, 32)).astype(BF)
        ring = then_y(h)
        ring.arrive()
        for place, z in enumerate(FIRST_X):
            zs[h, z] = ring.total(pl.ds(place * 32, 32)).astype(BF)
        for step in (2, 1, 3, 0):
            for zl_ in range(2):
                z_copy(h, zl_, (zh + step) % RING).start()

    def last(h):
        remote(zr.at[h], zr.at[h], zsend.at[h], zrecv.at[h], partner).wait_recv()
        done = zr[h, 0].astype(F32)
        for source in range(1, 8):
            done = done + zr[h, source].astype(F32)
        outw_ref[:, cols_of(h)] = done[:, :HD]
        outw_ref[:, cols_of(h, 1)] = done[:, HD:]

    def prompt_last(h):
        partner_terms(h)[1].wait_recv()
        for n in (1, 2):
            remote(rb.at[h, n], rb.at[h, n], tsend.at[h, 0], trecv.at[h, n], partner).wait_recv()

        @pl.loop(0, PLEN // 32)
        def _(i):
            rows = pl.ds(pl.multiple_of(i * 32, 32), 32)
            done = po[h, rows]
            for n in range(3):
                done = done + rb[h, n, rows].astype(F32)
            outp_ref[rows, cols_of(h)] = done[:, :HD]
            outp_ref[rows, cols_of(h, 1)] = done[:, HD:]

    relay(0)
    kv_load.wait()
    remote(xp_v, xp_v, xsend.at[0], xrecv.at[0], partner).wait_recv()

    @pl.loop(0, TILES)
    def _(t):
        xt_v[t, :, TOK:] = xp_v[t].T

    @pl.loop(0, KVH)
    def _(h):
        ready(h)

        @pl.loop(0, BLOCKS // 4)
        def _(i):
            @pl.when((i == 1) & (h >= 2))
            def _():
                third(h - 2)

            @pl.when((i == 1) & (h < KVH - 1))
            def _():
                relay(h + 1)

            block(h, i * 4 + 0)
            block(h, i * 4 + 1)
            block(h, i * 4 + 2)
            block(h, i * 4 + 3)

        g_copy(h).start()

        @pl.when(h >= 1)
        def _():
            second(h - 1)

        combine(h)
        product(h)
        back(h)

        @pl.when(h >= 2)
        def _():
            fourth(h - 2)

    third(KVH - 2)
    second(KVH - 1)
    fourth(KVH - 2)

    @pl.loop(0, KVH - 1)
    def _(h):
        prompt_last(h)

    third(KVH - 1)
    fourth(KVH - 1)
    prompt_last(KVH - 1)

    @pl.loop(0, KVH)
    def _(h):
        last(h)

    @pl.loop(0, KVH)
    def _(h):
        far = pk.at[h, pl.ds(0, 2)]
        remote(far, far, psend.at[h, 0], precv.at[h, 0], partner).wait_send()
        slot_copy(h, 1, 1, 2).wait_send()
        pass_copy(h).wait_send()
        g_copy(h).wait_send()
        for copy in term_copies(h) + partner_terms(h):
            copy.wait_send()
        for ring in (ring_y(h), ring_x(h), then_x(h), then_y(h)):
            ring.sent()
        remote(zr.at[h], zr.at[h], zsend.at[h], zrecv.at[h], partner).wait_send()
    remote(xp_v, xp_v, xsend.at[0], xrecv.at[0], partner).wait_send()


def hand_on(prompt_ref, weight_ref, outp_ref, outw_ref):
    outp_ref[...] = prompt_ref[...]
    outw_ref[...] = weight_ref[...]


def shards(resp_q, resp_kv, resp_out_grad, resp_x, prompt_kv, stretch_offset):
    any_spec = pl.BlockSpec(memory_space=pl.ANY)
    vmem = pl.BlockSpec(memory_space=pltpu.VMEM)

    def buffers(*shapes):
        return [pltpu.VMEM((KVH,) + shape + (PAIR,), BF) for shape in shapes]

    rings = []
    for parts in (len(FIRST_Y), len(FIRST_X)):
        rings += buffers((RING, parts * 128), (2, parts * 64), (2, parts * 128))
    for parts in (len(FIRST_Y), len(FIRST_X)):
        rings += buffers((RING, parts * 32), (3, parts * 32))

    dma = pltpu.SemaphoreType.DMA
    grads = pl.pallas_call(
        kernel,
        out_shape=(
            jax.ShapeDtypeStruct((PLEN, KVW), F32),
            jax.ShapeDtypeStruct((32, KVW), F32),
        ),
        in_specs=[pl.BlockSpec(memory_space=pltpu.SMEM)] + [any_spec] * 5,
        out_specs=(vmem, vmem),
        scratch_shapes=[
            pltpu.VMEM((KVH, TOK, GROUP * HD), BF),
            pltpu.VMEM((KVH, TOK, GROUP * HD), BF),
            pltpu.VMEM((TOK, KVW), BF),
            pltpu.VMEM((TILES, TOK, HD), BF),
            pltpu.VMEM((TILES, TOK, HD), BF),
            pltpu.VMEM((TILES, HD, 2 * TOK), BF),
            pltpu.VMEM((KVH, 5, 2, PLEN, HD), BF),
            pltpu.VMEM((BLOCKS, PLEN, PAIR), F32),
            pltpu.VMEM((KVH, PLEN, PAIR), F32),
            pltpu.VMEM((KVH, 2 * TOK, PAIR), BF),
            pltpu.VMEM((KVH, 4, PLEN, PAIR), BF),
            pltpu.VMEM((KVH, 3, PLEN, PAIR), BF),
            pltpu.VMEM((KVH, PLEN, PAIR), BF),
        ]
        + [
            pltpu.VMEM((KVH, RING, 32, PAIR), BF),
            pltpu.VMEM((KVH, 8, 32, PAIR), BF),
            dma((5, KVH)),
            dma((KVH, 3)), dma((KVH, 4)),
            dma((1,)), dma((1,)),
            dma((KVH,)), dma((KVH,)),
            dma((KVH, 4)), dma((KVH, 4)),
            dma((KVH,)), dma((KVH,)),
            dma((KVH, 4)), dma((KVH, 4, 6)),
        ]
        + rings,
        compiler_params=pltpu.CompilerParams(
            collective_id=0, has_side_effects=True, vmem_limit_bytes=56 * 1024 * 1024
        ),
        cost_estimate=pl.CostEstimate(
            flops=7_000_000_000, bytes_accessed=12_000_000, transcendentals=2_000_000
        ),
        name="attention_grads",
    )(stretch_offset, resp_q, resp_kv, resp_out_grad, resp_x, prompt_kv)
    return pl.pallas_call(
        hand_on,
        out_shape=(
            jax.ShapeDtypeStruct((PLEN, KVW), F32),
            jax.ShapeDtypeStruct((32, KVW), F32),
        ),
        in_specs=[vmem, vmem],
        out_specs=(vmem, vmem),
        name="hand_on",
    )(*grads)


def solution(mesh):
    return jax.shard_map(
        shards,
        mesh=mesh,
        in_specs=(
            P(("cuts", "dev"), None),
            P(("cuts", "dev"), None),
            P(("cuts", "dev"), None),
            P(("cuts", "dev"), None),
            P(("cuts", "dev"), None),
            P(("cuts", "dev")),
        ),
        out_specs=(P(("cuts", "dev"), None), P("dev", None)),
        check_vma=False,
    )
```
